512 devices in a mesh: grp: 64 (over z_lo, y, core), tile: 8 (over z_hi, x).
Axes of the slice: x: 4, y: 4, z: 16 (z_hi: 2, z_lo: 8; z = z_hi * 8 + z_lo), core: 2. Of those that a mesh axis runs over, the one named last changes fastest.
Arguments:
- points: float32 [3, 65536], P(None, ('grp', 'tile')), may hold values from 0 to 4
- probes: bfloat16 [8, 65536], P(None, ('grp', 'tile')), may hold values from -1 to 1
Outputs:
- products: float32 [3, 8, 65536], P(None, None, ('grp', 'tile'))
The draws below stay inside these ranges and needn't reach their ends.
All inputs are finite; a program needn't handle non-finite values.
Results may differ from the reference program's by a relative error of at most 0.0029.
Values may be sent and summed in bfloat16 or wider, within the bound.
No kernel may reach another device: no remote copies, remote signals or barrier semaphores. Data moves between devices by JAX's collectives and lax.ppermute only.
A program may use at most 64 MiB of HBM per device.

```python
import jax
import jax.numpy as jnp
from jax import lax

ROUNDS = 4
PROBES = 8
GROUP_PTS = 1024
NPTS = 65536
N_GRP = 64


def steps_of(stream_key, dims, pieces, least, high):
    gain, own = 1.0, jax.random.fold_in(stream_key, 6)
    for axis_at, parts in pieces:
        draws = jnp.exp(jax.random.uniform(jax.random.fold_in(own, axis_at), (parts,), jnp.float32, least / len(pieces), high / len(pieces)))
        gain = gain * jnp.repeat(draws, dims[axis_at] // parts).reshape([-1 if axis == axis_at else 1 for axis in range(len(dims))])
    return gain


def normal_values(key, dims, spread, limit, shards=(), held_as=jnp.bfloat16):
    values = spread * jax.random.normal(key, dims, jnp.float32)
    if shards:
        values = values * steps_of(key, dims, shards, -0.22, 0.18)
    return jnp.clip(values, -limit, limit).astype(held_as)


def setup_inputs(seed: int = 0) -> dict:
    keys = jax.random.split(jax.random.key(seed), 3)
    return {
        "points": jnp.clip(4.0 * jax.random.uniform(keys[0], (3, NPTS), jnp.float32) ** steps_of(keys[0], (3, NPTS), ((1, 512),), -0.2, 0.2), 0.0, 4.0),
        "probes": normal_values(keys[1], (PROBES, NPTS), (2 * ROUNDS * GROUP_PTS // 256) ** -0.5, 1.0, ((1, 512),)),
    }


def tile_kernels(row_points, col_points):
    diffs = row_points[:, :, None] - col_points[:, None, :]
    flat_q = (diffs[0] * diffs[0] + diffs[1] * diffs[1]) / (0.35 * 0.35)
    depth_q = diffs[2] * diffs[2] / (0.25 * 0.25)
    scaled = jnp.sqrt(3.0 * (flat_q + depth_q) + 1e-06)
    decay = 1.3 * jnp.exp(-scaled)
    stacked = jnp.stack([(1.0 + scaled) * decay, 3.0 * flat_q * decay, 3.0 * depth_q * decay])
    return stacked.astype(jnp.bfloat16)

def reference(points, probes):
    grouped_pts = points.reshape(3, N_GRP, GROUP_PTS).transpose(1, 0, 2)
    grouped_probe = probes.reshape(PROBES, N_GRP, GROUP_PTS).transpose(1, 0, 2)
    result_sum = jnp.zeros((N_GRP, 3, PROBES, GROUP_PTS), jnp.float32)

    def one_pair(items):
        row_pts, row_probe, col_pts, col_probe = items
        kernels = tile_kernels(row_pts, col_pts).astype(jnp.float32)
        forward = jnp.einsum('kmn,pn->kpm', kernels, col_probe.astype(jnp.float32), precision=lax.Precision.HIGHEST)
        mirrored = jnp.einsum('kmn,pm->kpn', kernels, row_probe.astype(jnp.float32), precision=lax.Precision.HIGHEST)
        return (forward, mirrored)
    for offset in range(1, ROUNDS + 1):
        far_pts = jnp.roll(grouped_pts, -offset, axis=0)
        far_probe = jnp.roll(grouped_probe, -offset, axis=0)
        forward, mirrored = lax.map(one_pair, (grouped_pts, grouped_probe, far_pts, far_probe))
        result_sum = result_sum + forward + jnp.roll(mirrored, offset, axis=0)
    return result_sum.transpose(1, 2, 0, 3).reshape(3, PROBES, NPTS)
```

```python
import math

import jax
import jax.numpy as jnp
import numpy as np
from jax import lax
from jax.experimental import pallas as pl
from jax.experimental.pallas import tpu as pltpu
from jax.sharding import PartitionSpec as P

ROUNDS = 4
PLANE_GROUPS = 8
PLANES = 16
ROW_TILES = 4
LANES = 128
ROW_CHUNK = 16
COL_CHUNK = 256
SCALES = np.array([[math.sqrt(3) / 0.35], [math.sqrt(3) / 0.35], [math.sqrt(3) / 0.25]], np.float32)


def device_at(plane, member, column):
    return ((plane % 8) * PLANE_GROUPS + member) * 8 + (plane // 8) * ROW_TILES + column


def next_plane(block):
    route = []
    for plane in range(PLANES):
        for member in range(PLANE_GROUPS):
            step = -1 if member < PLANE_GROUPS // 2 else 1
            for column in range(ROW_TILES):
                route.append(
                    (
                        device_at(plane, member, column),
                        device_at((plane + step) % PLANES, member, column),
                    )
                )
    return lax.ppermute(block, ("grp", "tile"), route)


def other_half(block):
    return lax.ppermute(block, "tile", [(i, i ^ 4) for i in range(8)])


def within_plane(block):
    planes = [
        [device_at(plane, m, c) for m in range(PLANE_GROUPS) for c in range(ROW_TILES)]
        for plane in range(PLANES)
    ]
    copies = jnp.broadcast_to(block[None], (len(planes[0]),) + block.shape)
    return lax.all_to_all(copies, ("grp", "tile"), 0, 0, axis_index_groups=planes)


def pack(points, probes):
    scaled = (points - 2.0) * SCALES
    lead = lax.reduce_precision(scaled, 8, 7)
    rest = scaled - lead
    unused = jnp.zeros((2, points.shape[1]), jnp.bfloat16)
    return jnp.concatenate(
        [probes, lead.astype(jnp.bfloat16), rest.astype(jnp.bfloat16), unused], 0
    )


def products_kernel(own_ref, far_ref, out_ref, rows_ref, tile_ref):
    own = own_ref[...].astype(jnp.float32)
    coords = jnp.concatenate([own[8:11] + own[11:14], jnp.zeros((5, LANES), jnp.float32)], 0)
    upright = jnp.transpose(coords)
    for k in range(3):
        rows_ref[k] = jnp.broadcast_to(upright[:, k : k + 1], (LANES, LANES))
    member = lax.rem(lax.axis_index("grp"), PLANE_GROUPS)
    blocks = COL_CHUNK // LANES

    def tiles(cols, at):
        parts = []
        for col in cols:
            d = [rows_ref[k, pl.ds(at, ROW_CHUNK), :] - col[k] for k in range(3)]
            flat_q = d[0] * d[0] + d[1] * d[1]
            depth_q = d[2] * d[2]
            total = (flat_q + depth_q) + 1e-6
            scaled = total * lax.rsqrt(total)
            decay = jnp.exp2(math.log2(1.3) - scaled * math.log2(math.e))
            parts.append(((1.0 + scaled) * decay, flat_q * decay, depth_q * decay))
        return [jnp.concatenate([p[k] for p in parts], 1).astype(jnp.bfloat16) for k in range(3)]

    def step(n, total):
        at = member + jnp.where(n < ROUNDS, n - ROUNDS, n - ROUNDS + 1)
        sender = lax.rem(at + PLANE_GROUPS, PLANE_GROUPS)
        kind = jnp.where((at >= 0) & (at < PLANE_GROUPS), 0, 1)
        for half in range(2):
            for part in range(ROW_TILES // blocks):
                cells = [
                    far_ref[sender * ROW_TILES + part * blocks + w, half * 2 + kind]
                    for w in range(blocks)
                ]
                probe = jnp.concatenate([cell[0:8] for cell in cells], 1)
                wide = [cell.astype(jnp.float32) for cell in cells]
                cols = [
                    [
                        jnp.broadcast_to(f[8 + k : 9 + k] + f[11 + k : 12 + k], (ROW_CHUNK, LANES))
                        for k in range(3)
                    ]
                    for f in wide
                ]
                slot = half * 2 + part
                for start in range(0, LANES, ROW_CHUNK):
                    made = tiles(cols, start)
                    for k in range(3):
                        tile_ref[slot, pl.ds(k * LANES + start, ROW_CHUNK), :] = made[k]
                total = total + lax.dot_general(
                    probe,
                    tile_ref[slot],
                    (((1,), (1,)), ((), ())),
                    preferred_element_type=jnp.float32,
                )
        return total

    total = lax.fori_loop(0, 2 * ROUNDS, step, jnp.zeros((8, 3 * LANES), jnp.float32))
    for k in range(3):
        out_ref[k] = total[:, k * LANES : (k + 1) * LANES]


def products(own, far):
    return pl.pallas_call(
        products_kernel,
        out_shape=jax.ShapeDtypeStruct((3, 8, LANES), jnp.float32),
        in_specs=[pl.BlockSpec(memory_space=pltpu.VMEM)] * 2,
        out_specs=pl.BlockSpec(memory_space=pltpu.VMEM),
        scratch_shapes=[
            pltpu.VMEM((3, LANES, LANES), jnp.float32),
            pltpu.VMEM((4, 3 * LANES, COL_CHUNK), jnp.bfloat16),
        ],
        compiler_params=pltpu.CompilerParams(vmem_limit_bytes=32 * 2**20),
    )(own, far)


def body(points, probes):
    own = pack(points, probes)
    held = jnp.stack([own, next_plane(own)])
    held = jnp.concatenate([held, other_half(held)], 0)
    return products(own, within_plane(held))


def solution(mesh):
    return jax.shard_map(
        body,
        mesh=mesh,
        in_specs=(P(None, ("grp", "tile")), P(None, ("grp", "tile"))),
        out_specs=P(None, None, ("grp", "tile")),
        check_vma=False,
    )
```

```python
import math

import jax
import jax.numpy as jnp
from jax import lax
from jax.experimental import pallas as pl
from jax.experimental.pallas import tpu as pltpu
from jax.sharding import PartitionSpec as P

ROUNDS = 4
PLANE_GROUPS = 8
PLANES = 16
ROW_TILES = 4
LANES = 128
ROWS = 24
ROW_CHUNK = 16
COL_CHUNK = 256
SCALES = (math.sqrt(3) / 0.35, math.sqrt(3) / 0.35, math.sqrt(3) / 0.25)


def device_at(plane, member, column):
    return ((plane % 8) * PLANE_GROUPS + member) * 8 + (plane // 8) * ROW_TILES + column


def across_planes(block):
    sets = []
    for plane in range(PLANES // 2):
        for member in range(4, PLANE_GROUPS):
            for column in range(ROW_TILES):
                lower = (member + 2) % 4
                near = [device_at(plane, member, column), device_at(plane + 1, lower, column)]
                far = [
                    device_at(plane + 8, member, column),
                    device_at((plane + 9) % PLANES, lower, column),
                ]
                sets.append(near + far if plane == 7 else far + near)
    copies = jnp.broadcast_to(block[None], (4,) + block.shape)
    return lax.all_to_all(copies, ("grp", "tile"), 0, 0, axis_index_groups=sets)


def within_plane(block):
    planes = [
        [
            device_at(plane, 2 * m + core, c)
            for m in reversed(range(PLANE_GROUPS // 2))
            for c in reversed(range(ROW_TILES))
        ]
        for plane in range(PLANES)
        for core in range(2)
    ]
    copies = jnp.broadcast_to(block[None], (len(planes[0]),) + block.shape)
    return lax.all_to_all(copies, ("grp", "tile"), 0, 0, axis_index_groups=planes)


def other_core(block):
    return lax.ppermute(block, "grp", [(i, i ^ 1) for i in range(64)])


def pack_kernel(points_ref, probes_ref, out_ref):
    rest = points_ref[...]
    parts = []
    for _ in range(3):
        part = rest.astype(jnp.bfloat16).astype(jnp.float32)
        parts += [part, jnp.zeros((1, LANES), jnp.float32)]
        rest = rest - part
    probes = probes_ref[...].astype(jnp.float32)
    out_ref[...] = jnp.concatenate(
        [probes] + parts + [jnp.zeros((4, LANES), jnp.float32)], 0
    ).astype(jnp.bfloat16)


def pack(points, probes):
    return pl.pallas_call(
        pack_kernel,
        out_shape=jax.ShapeDtypeStruct((ROWS, LANES), jnp.bfloat16),
        in_specs=[pl.BlockSpec(memory_space=pltpu.VMEM)] * 2,
        out_specs=pl.BlockSpec(memory_space=pltpu.VMEM),
    )(points, probes)


def unpack(block):
    wide = block.astype(jnp.float32)
    return wide[0:8], (wide[8:11] + wide[12:15]) + wide[16:19]


def products_kernel(first, *refs):
    if first:
        own_ref, far_ref, out_ref, rows_ref, tile_ref = refs
    else:
        own_ref, far_ref, before_ref, out_ref, rows_ref, tile_ref = refs
    own = unpack(own_ref[...])[1]
    centre = own[:, 0:1]
    upright = jnp.transpose(jnp.concatenate([own, jnp.zeros((5, LANES), jnp.float32)], 0))
    for k in range(3):
        column = (upright[:, k : k + 1] - centre[k : k + 1]) * SCALES[k]
        rows_ref[k] = jnp.broadcast_to(column, (LANES, LANES))
    member = lax.rem(lax.axis_index("grp"), PLANE_GROUPS)
    blocks = COL_CHUNK // LANES

    def tiles(cols, at):
        parts = []
        for col in cols:
            d = [rows_ref[k, pl.ds(at, ROW_CHUNK), :] - col[k] for k in range(3)]
            flat_q = d[0] * d[0] + d[1] * d[1]
            depth_q = d[2] * d[2]
            total = (flat_q + depth_q) + 1e-6
            scaled = total * lax.rsqrt(total)
            decay = jnp.exp2(math.log2(1.3) - scaled * math.log2(math.e))
            parts.append(((1.0 + scaled) * decay, flat_q * decay, depth_q * decay))
        return [jnp.concatenate([p[k] for p in parts], 1).astype(jnp.bfloat16) for k in range(3)]

    if first:
        total = jnp.zeros((8, 3 * LANES), jnp.float32)
    else:
        total = jnp.concatenate([before_ref[k] for k in range(3)], 1)
    slot = 0
    for offset in (-4, -2, 2, 4) if first else (-3, -1, 1, 3):
        wanted = member + offset
        group = lax.rem(wanted + PLANE_GROUPS, PLANE_GROUPS)
        inside = (wanted >= 0) & (wanted < PLANE_GROUPS)
        twin = lax.rem(group + 2, 4) + jnp.where(group < 4, 4, 0)
        place = (PLANE_GROUPS - 1 - jnp.where(inside, group, twin)) // 2
        kind = jnp.where(group < 4, 1, 0)
        for half in range(2):
            for part in range(ROW_TILES // blocks):
                cells = [
                    unpack(far_ref[place * ROW_TILES + part * blocks + w, 2 * half + kind])
                    for w in range(blocks)
                ]
                probe = jnp.concatenate([cell[0] for cell in cells], 1).astype(jnp.bfloat16)
                cols = [
                    [
                        jnp.broadcast_to(
                            (cell[1][k : k + 1] - centre[k : k + 1]) * SCALES[k],
                            (ROW_CHUNK, LANES),
                        )
                        for k in range(3)
                    ]
                    for cell in cells
                ]
                for start in range(0, LANES, ROW_CHUNK):
                    made = tiles(cols, start)
                    for k in range(3):
                        tile_ref[slot % 4, pl.ds(k * LANES + start, ROW_CHUNK), :] = made[k]
                total = total + lax.dot_general(
                    probe,
                    tile_ref[slot % 4],
                    (((1,), (1,)), ((), ())),
                    preferred_element_type=jnp.float32,
                )
                slot += 1
    for k in range(3):
        out_ref[k] = total[:, k * LANES : (k + 1) * LANES]


def products(own, far, before=None):
    operands = (own, far) if before is None else (own, far, before)
    return pl.pallas_call(
        lambda *refs: products_kernel(before is None, *refs),
        out_shape=jax.ShapeDtypeStruct((3, 8, LANES), jnp.float32),
        in_specs=[pl.BlockSpec(memory_space=pltpu.VMEM)] * len(operands),
        out_specs=pl.BlockSpec(memory_space=pltpu.VMEM),
        scratch_shapes=[
            pltpu.VMEM((3, LANES, LANES), jnp.float32),
            pltpu.VMEM((4, 3 * LANES, COL_CHUNK), jnp.bfloat16),
        ],
        compiler_params=pltpu.CompilerParams(vmem_limit_bytes=32 * 2**20),
        cost_estimate=pl.CostEstimate(flops=30_000_000, bytes_accessed=500_000, transcendentals=1_000_000),
    )(*operands)


def body(points, probes):
    own = pack(points, probes)
    same = within_plane(across_planes(own))
    swapped = other_core(same)
    return products(own, swapped, products(own, same))


def solution(mesh):
    return jax.shard_map(
        body,
        mesh=mesh,
        in_specs=(P(None, ("grp", "tile")), P(None, ("grp", "tile"))),
        out_specs=P(None, None, ("grp", "tile")),
        check_vma=False,
    )
```

```python
import math

import jax
import jax.numpy as jnp
from jax import lax
from jax.experimental import pallas as pl
from jax.experimental.pallas import tpu as pltpu
from jax.sharding import PartitionSpec as P

ROUNDS = 4
PLANE_GROUPS = 8
PLANES = 16
ROW_TILES = 4
LANES = 128
ROWS = 24
ROW_CHUNK = 16
COL_CHUNK = 256
SCALES = (math.sqrt(3) / 0.35, math.sqrt(3) / 0.35, math.sqrt(3) / 0.25)


def device_at(plane, member, column):
    return ((plane % 8) * PLANE_GROUPS + member) * 8 + (plane // 8) * ROW_TILES + column


def across_planes(copies):
    sets = []
    for plane in range(PLANES // 2):
        for member in range(4, PLANE_GROUPS):
            for column in range(ROW_TILES):
                lower = (member + 2) % 4
                near = [device_at(plane, member, column), device_at(plane + 1, lower, column)]
                far = [
                    device_at(plane + 8, member, column),
                    device_at((plane + 9) % PLANES, lower, column),
                ]
                sets.append(near + far if plane == 7 else far + near)
    return lax.all_to_all(copies, ("grp", "tile"), 0, 0, axis_index_groups=sets)


def within_plane(block):
    planes = [
        [
            device_at(plane, 2 * m + core, c)
            for m in range(PLANE_GROUPS // 2)
            for c in (2, 3, 0, 1)
        ]
        for plane in range(PLANES)
        for core in range(2)
    ]
    copies = jnp.broadcast_to(block[None], (len(planes[0]),) + block.shape)
    return lax.all_to_all(copies, ("grp", "tile"), 0, 0, axis_index_groups=planes)


def other_core(block):
    return lax.ppermute(block, "grp", [(i, i ^ 1) for i in range(64)])


def pack_kernel(points_ref, probes_ref, out_ref):
    rest = points_ref[...]
    parts = []
    for _ in range(3):
        part = rest.astype(jnp.bfloat16).astype(jnp.float32)
        parts += [part, jnp.zeros((1, LANES), jnp.float32)]
        rest = rest - part
    probes = probes_ref[...].astype(jnp.float32)
    packed = jnp.concatenate(
        [probes] + parts + [jnp.zeros((4, LANES), jnp.float32)], 0
    ).astype(jnp.bfloat16)
    for copy in range(4):
        out_ref[copy] = packed


def pack(points, probes):
    points = pltpu.with_memory_space_constraint(points, pltpu.HBM)
    probes = pltpu.with_memory_space_constraint(probes, pltpu.HBM)
    return pl.pallas_call(
        pack_kernel,
        out_shape=jax.ShapeDtypeStruct((4, ROWS, LANES), jnp.bfloat16),
        in_specs=[pl.BlockSpec(memory_space=pltpu.VMEM)] * 2,
        out_specs=pl.BlockSpec(memory_space=pltpu.VMEM),
        compiler_params=pltpu.CompilerParams(vmem_limit_bytes=2**20),
    )(points, probes)


def unpack(block):
    wide = block.astype(jnp.float32)
    return wide[0:8], (wide[8:11] + wide[12:15]) + wide[16:19]


def products_kernel(first, *refs):
    if first:
        own_ref, far_ref, out_ref, rows_ref, tile_ref = refs
    else:
        own_ref, far_ref, before_ref, out_ref, rows_ref, tile_ref = refs
    own = unpack(own_ref[0])[1]
    centre = own[:, 0:1]
    upright = jnp.transpose(jnp.concatenate([own, jnp.zeros((5, LANES), jnp.float32)], 0))
    for k in range(3):
        column = (upright[:, k : k + 1] - centre[k : k + 1]) * SCALES[k]
        rows_ref[k] = jnp.broadcast_to(column, (LANES, LANES))
    member = lax.rem(lax.axis_index("grp"), PLANE_GROUPS)
    blocks = COL_CHUNK // LANES

    def tiles(cols, at):
        parts = []
        for col in cols:
            d = [rows_ref[k, pl.ds(at, ROW_CHUNK), :] - col[k] for k in range(3)]
            flat_q = d[0] * d[0] + d[1] * d[1]
            depth_q = d[2] * d[2]
            total = (flat_q + depth_q) + 1e-6
            scaled = total * lax.rsqrt(total)
            decay = jnp.exp2(math.log2(1.3) - scaled * math.log2(math.e))
            parts.append(((1.0 + scaled) * decay, flat_q * decay, depth_q * decay))
        return [jnp.concatenate([p[k] for p in parts], 1).astype(jnp.bfloat16) for k in range(3)]

    if first:
        total = jnp.zeros((8, 3 * LANES), jnp.float32)
    else:
        total = jnp.concatenate([before_ref[k] for k in range(3)], 1)
    slot = 0
    for offset in (-4, -2, 2, 4) if first else (-3, -1, 1, 3):
        wanted = member + offset
        group = lax.rem(wanted + PLANE_GROUPS, PLANE_GROUPS)
        inside = (wanted >= 0) & (wanted < PLANE_GROUPS)
        twin = lax.rem(group + 2, 4) + jnp.where(group < 4, 4, 0)
        place = jnp.where(inside, group, twin) // 2
        kind = jnp.where(group < 4, 1, 0)
        for half in range(2):
            for part in range(ROW_TILES // blocks):
                cells = [
                    unpack(far_ref[place * ROW_TILES + part * blocks + w, 2 * half + kind])
                    for w in range(blocks)
                ]
                probe = jnp.concatenate([cell[0] for cell in cells], 1).astype(jnp.bfloat16)
                cols = [
                    [
                        jnp.broadcast_to(
                            (cell[1][k : k + 1] - centre[k : k + 1]) * SCALES[k],
                            (ROW_CHUNK, LANES),
                        )
                        for k in range(3)
                    ]
                    for cell in cells
                ]
                for start in range(0, LANES, ROW_CHUNK):
                    made = tiles(cols, start)
                    for k in range(3):
                        tile_ref[slot % 4, pl.ds(k * LANES + start, ROW_CHUNK), :] = made[k]
                total = total + lax.dot_general(
                    probe,
                    tile_ref[slot % 4],
                    (((1,), (1,)), ((), ())),
                    preferred_element_type=jnp.float32,
                )
                slot += 1
    for k in range(3):
        out_ref[k] = total[:, k * LANES : (k + 1) * LANES]


def products(own, far, before=None):
    operands = (own, far) if before is None else (own, far, before)
    return pl.pallas_call(
        lambda *refs: products_kernel(before is None, *refs),
        out_shape=jax.ShapeDtypeStruct((3, 8, LANES), jnp.float32),
        in_specs=[pl.BlockSpec(memory_space=pltpu.VMEM)] * len(operands),
        out_specs=pl.BlockSpec(memory_space=pltpu.VMEM),
        scratch_shapes=[
            pltpu.VMEM((3, LANES, LANES), jnp.float32),
            pltpu.VMEM((4, 3 * LANES, COL_CHUNK), jnp.bfloat16),
        ],
        compiler_params=pltpu.CompilerParams(vmem_limit_bytes=32 * 2**20),
        cost_estimate=pl.CostEstimate(flops=30_000_000, bytes_accessed=500_000, transcendentals=1_000_000),
    )(*operands)


def body(points, probes):
    own = pack(points, probes)
    same = within_plane(across_planes(own))
    swapped = other_core(same)
    return products(own, swapped, products(own, same))


def solution(mesh):
    return jax.shard_map(
        body,
        mesh=mesh,
        in_specs=(P(None, ("grp", "tile")), P(None, ("grp", "tile"))),
        out_specs=P(None, None, ("grp", "tile")),
        check_vma=False,
    )
```

```python
import math

import jax
import jax.numpy as jnp
from jax import lax
from jax.experimental import pallas as pl
from jax.experimental.pallas import tpu as pltpu
from jax.sharding import PartitionSpec as P

ROUNDS = 4
PLANE_GROUPS = 8
PLANES = 16
ROW_TILES = 4
LANES = 128
ROWS = 24
SET_ROWS = 72
ROW_CHUNK = 16
COL_CHUNK = 256
SCALES = (math.sqrt(3) / 0.35, math.sqrt(3) / 0.35, math.sqrt(3) / 0.25)


def device_at(plane, member, column):
    return ((plane % 8) * PLANE_GROUPS + member) * 8 + (plane // 8) * ROW_TILES + column


def across_planes(copies):
    sets = []
    for plane in range(PLANES // 2):
        for member in range(4, PLANE_GROUPS):
            for column in range(ROW_TILES):
                lower = (member + 2) % 4
                near = [device_at(plane, member, column), device_at(plane + 1, lower, column)]
                far = [
                    device_at(plane + 8, member, column),
                    device_at((plane + 9) % PLANES, lower, column),
                ]
                sets.append(near + far if plane == 7 else far + near)
    return lax.all_to_all(copies, ("grp", "tile"), 0, 0, axis_index_groups=sets)


def within_plane(copies):
    planes = [
        [
            device_at(plane, 2 * m + core, c)
            for m in range(PLANE_GROUPS // 2)
            for c in (2, 3, 0, 1)
        ]
        for plane in range(PLANES)
        for core in range(2)
    ]
    return lax.all_to_all(copies, ("grp", "tile"), 0, 0, axis_index_groups=planes)


def other_core(block):
    return lax.ppermute(block, "grp", [(i, i ^ 1) for i in range(64)])


def pack_kernel(points_ref, probes_ref, out_ref):
    rest = points_ref[...]
    parts = []
    for _ in range(3):
        part = rest.astype(jnp.bfloat16).astype(jnp.float32)
        parts += [part, jnp.zeros((1, LANES), jnp.float32)]
        rest = rest - part
    probes = probes_ref[...].astype(jnp.float32)
    packed = jnp.concatenate(
        [probes] + parts + [jnp.zeros((4, LANES), jnp.float32)], 0
    ).astype(jnp.bfloat16)
    for copy in range(4):
        out_ref[copy] = packed


def pack(points, probes):
    points = pltpu.with_memory_space_constraint(points, pltpu.HBM)
    probes = pltpu.with_memory_space_constraint(probes, pltpu.HBM)
    return pl.pallas_call(
        pack_kernel,
        out_shape=jax.ShapeDtypeStruct((4, ROWS, LANES), jnp.bfloat16),
        in_specs=[pl.BlockSpec(memory_space=pltpu.VMEM)] * 2,
        out_specs=pl.BlockSpec(memory_space=pltpu.VMEM),
        compiler_params=pltpu.CompilerParams(vmem_limit_bytes=2**20),
    )(points, probes)


def gather_kernel(set_ref, out_ref):
    wide = [set_ref[b].astype(jnp.float32) for b in (0, 2, 1, 3)]
    packed = jnp.concatenate(
        [block[0:8] for block in wide]
        + [block[at : at + 3] for at in (8, 12, 16) for block in wide]
        + [jnp.zeros((4, LANES), jnp.float32)],
        0,
    ).astype(jnp.bfloat16)
    for copy in range(out_ref.shape[0]):
        out_ref[copy] = packed


def gather(blocks):
    return pl.pallas_call(
        gather_kernel,
        out_shape=jax.ShapeDtypeStruct((16, SET_ROWS, LANES), jnp.bfloat16),
        in_specs=[pl.BlockSpec(memory_space=pltpu.VMEM)],
        out_specs=pl.BlockSpec(memory_space=pltpu.VMEM),
        compiler_params=pltpu.CompilerParams(vmem_limit_bytes=2**20),
    )(blocks)


def unpack(message, kind):
    wide = message.astype(jnp.float32)
    coords = (wide[32:44] + wide[44:56]) + wide[56:68]
    first = kind == 0
    return jnp.where(first, wide[0:16], wide[16:32]), jnp.where(first, coords[0:6], coords[6:12])


def products_kernel(first, *refs):
    if first:
        own_ref, far_ref, out_ref, rows_ref, tile_ref = refs
    else:
        own_ref, far_ref, before_ref, out_ref, rows_ref, tile_ref = refs
    wide = own_ref[0].astype(jnp.float32)
    own = (wide[8:11] + wide[12:15]) + wide[16:19]
    centre = own[:, 0:1]
    upright = jnp.transpose(jnp.concatenate([own, jnp.zeros((5, LANES), jnp.float32)], 0))
    for k in range(3):
        column = (upright[:, k : k + 1] - centre[k : k + 1]) * SCALES[k]
        rows_ref[k] = jnp.broadcast_to(column, (LANES, LANES))
    member = lax.rem(lax.axis_index("grp"), PLANE_GROUPS)
    blocks = COL_CHUNK // LANES

    def tiles(cols, at):
        parts = []
        for col in cols:
            d = [rows_ref[k, pl.ds(at, ROW_CHUNK), :] - col[k] for k in range(3)]
            flat_q = d[0] * d[0] + d[1] * d[1]
            depth_q = d[2] * d[2]
            total = (flat_q + depth_q) + 1e-6
            scaled = total * lax.rsqrt(total)
            decay = jnp.exp2(math.log2(1.3) - scaled * math.log2(math.e))
            parts.append(((1.0 + scaled) * decay, flat_q * decay, depth_q * decay))
        return [jnp.concatenate([p[k] for p in parts], 1).astype(jnp.bfloat16) for k in range(3)]

    if first:
        total = jnp.zeros((8, 3 * LANES), jnp.float32)
    else:
        total = jnp.concatenate([before_ref[k] for k in range(3)], 1)
    slot = 0
    for offset in (-4, -2, 2, 4) if first else (-3, -1, 1, 3):
        wanted = member + offset
        group = lax.rem(wanted + PLANE_GROUPS, PLANE_GROUPS)
        inside = (wanted >= 0) & (wanted < PLANE_GROUPS)
        twin = lax.rem(group + 2, 4) + jnp.where(group < 4, 4, 0)
        place = jnp.where(inside, group, twin) // 2
        kind = jnp.where(group < 4, 1, 0)
        for part in range(ROW_TILES // blocks):
            cells = [
                unpack(far_ref[place * ROW_TILES + part * blocks + w], kind) for w in range(blocks)
            ]
            for half in range(2):
                probe = jnp.concatenate(
                    [cell[0][half * 8 : half * 8 + 8] for cell in cells], 1
                ).astype(jnp.bfloat16)
                cols = [
                    [
                        jnp.broadcast_to(
                            (cell[1][half * 3 + k : half * 3 + k + 1] - centre[k : k + 1])
                            * SCALES[k],
                            (ROW_CHUNK, LANES),
                        )
                        for k in range(3)
                    ]
                    for cell in cells
                ]
                for start in range(0, LANES, ROW_CHUNK):
                    made = tiles(cols, start)
                    for k in range(3):
                        tile_ref[slot % 4, pl.ds(k * LANES + start, ROW_CHUNK), :] = made[k]
                total = total + lax.dot_general(
                    probe,
                    tile_ref[slot % 4],
                    (((1,), (1,)), ((), ())),
                    preferred_element_type=jnp.float32,
                )
                slot += 1
    for k in range(3):
        out_ref[k] = total[:, k * LANES : (k + 1) * LANES]


def products(own, far, before=None):
    operands = (own, far) if before is None else (own, far, before)
    return pl.pallas_call(
        lambda *refs: products_kernel(before is None, *refs),
        out_shape=jax.ShapeDtypeStruct((3, 8, LANES), jnp.float32),
        in_specs=[pl.BlockSpec(memory_space=pltpu.VMEM)] * len(operands),
        out_specs=pl.BlockSpec(memory_space=pltpu.VMEM),
        scratch_shapes=[
            pltpu.VMEM((3, LANES, LANES), jnp.float32),
            pltpu.VMEM((4, 3 * LANES, COL_CHUNK), jnp.bfloat16),
        ],
        compiler_params=pltpu.CompilerParams(vmem_limit_bytes=32 * 2**20),
        cost_estimate=pl.CostEstimate(flops=30_000_000, bytes_accessed=500_000, transcendentals=1_000_000),
    )(*operands)


def body(points, probes):
    own = pack(points, probes)
    same = within_plane(gather(across_planes(own)))
    swapped = other_core(same)
    return products(own, swapped, products(own, same))


def solution(mesh):
    return jax.shard_map(
        body,
        mesh=mesh,
        in_specs=(P(None, ("grp", "tile")), P(None, ("grp", "tile"))),
        out_specs=P(None, None, ("grp", "tile")),
        check_vma=False,
    )
```

```python
import math

import jax
import jax.numpy as jnp
from jax import lax
from jax.experimental import pallas as pl
from jax.experimental.pallas import tpu as pltpu
from jax.sharding import PartitionSpec as P

ROUNDS = 4
PLANE_GROUPS = 8
PLANES = 16
ROW_TILES = 4
LANES = 128
ROWS = 24
SET_ROWS = 72
ROW_CHUNK = 16
COL_CHUNK = 256
SCALES = (math.sqrt(3) / 0.35, math.sqrt(3) / 0.35, math.sqrt(3) / 0.25)


def device_at(plane, member, column):
    return ((plane % 8) * PLANE_GROUPS + member) * 8 + (plane // 8) * ROW_TILES + column


def across_planes(copies):
    sets = []
    for plane in range(PLANES // 2):
        for member in range(4, PLANE_GROUPS):
            for column in range(ROW_TILES):
                lower = (member + 2) % 4
                near = [device_at(plane, member, column), device_at(plane + 1, lower, column)]
                far = [
                    device_at(plane + 8, member, column),
                    device_at((plane + 9) % PLANES, lower, column),
                ]
                sets.append(near + far if plane == 7 else far + near)
    return lax.all_to_all(copies, ("grp", "tile"), 0, 0, axis_index_groups=sets)


def within_plane(copies):
    planes = [
        [
            device_at(plane, 2 * m + core, c)
            for m in range(PLANE_GROUPS // 2)
            for c in (2, 3, 0, 1)
        ]
        for plane in range(PLANES)
        for core in range(2)
    ]
    return lax.all_to_all(copies, ("grp", "tile"), 0, 0, axis_index_groups=planes)


def other_core(block):
    return lax.ppermute(block, "grp", [(i, i ^ 1) for i in range(64)])


def pack_kernel(points_ref, probes_ref, out_ref):
    rest = points_ref[...]
    parts = []
    for _ in range(3):
        part = rest.astype(jnp.bfloat16).astype(jnp.float32)
        parts += [part, jnp.zeros((1, LANES), jnp.float32)]
        rest = rest - part
    probes = probes_ref[...].astype(jnp.float32)
    packed = jnp.concatenate(
        [probes] + parts + [jnp.zeros((4, LANES), jnp.float32)], 0
    ).astype(jnp.bfloat16)
    for copy in range(4):
        out_ref[copy] = packed


def pack(points, probes):
    points = pltpu.with_memory_space_constraint(points, pltpu.HBM)
    probes = pltpu.with_memory_space_constraint(probes, pltpu.HBM)
    return pl.pallas_call(
        pack_kernel,
        out_shape=jax.ShapeDtypeStruct((4, ROWS, LANES), jnp.bfloat16),
        in_specs=[pl.BlockSpec(memory_space=pltpu.VMEM)] * 2,
        out_specs=pl.BlockSpec(memory_space=pltpu.VMEM),
        compiler_params=pltpu.CompilerParams(vmem_limit_bytes=2**20),
    )(points, probes)


def gather_kernel(set_ref, out_ref):
    wide = [set_ref[b].astype(jnp.float32) for b in (0, 2, 1, 3)]
    packed = jnp.concatenate(
        [block[0:8] for block in wide]
        + [block[at : at + 3] for at in (8, 12, 16) for block in wide]
        + [jnp.zeros((4, LANES), jnp.float32)],
        0,
    ).astype(jnp.bfloat16)
    for copy in range(out_ref.shape[0]):
        out_ref[copy] = packed


def gather(blocks):
    return pl.pallas_call(
        gather_kernel,
        out_shape=jax.ShapeDtypeStruct((16, SET_ROWS, LANES), jnp.bfloat16),
        in_specs=[pl.BlockSpec(memory_space=pltpu.VMEM)],
        out_specs=pl.BlockSpec(memory_space=pltpu.VMEM),
        compiler_params=pltpu.CompilerParams(vmem_limit_bytes=2**20),
    )(blocks)


def unpack(message, kind):
    wide = message.astype(jnp.float32)
    coords = (wide[32:44] + wide[44:56]) + wide[56:68]
    first = kind == 0
    return jnp.where(first, wide[0:16], wide[16:32]), jnp.where(first, coords[0:6], coords[6:12])


def early_kernel(own_ref, far_ref, out_ref, rows_ref, tile_ref):
    core = lax.rem(lax.axis_index("grp"), 2)

    @pl.when(core == 1)
    def _():
        products_kernel(True, own_ref, far_ref, out_ref, rows_ref, tile_ref)

    @pl.when(core == 0)
    def _():
        out_ref[...] = jnp.zeros(out_ref.shape, jnp.float32)


def late_kernel(own_ref, far_ref, before_ref, out_ref, rows_ref, tile_ref):
    core = lax.rem(lax.axis_index("grp"), 2)

    @pl.when(core == 0)
    def _():
        products_kernel(True, own_ref, far_ref, out_ref, rows_ref, tile_ref)

    @pl.when(core == 1)
    def _():
        out_ref[...] = before_ref[...]


def products_kernel(first, *refs):
    if first:
        own_ref, far_ref, out_ref, rows_ref, tile_ref = refs
    else:
        own_ref, far_ref, before_ref, out_ref, rows_ref, tile_ref = refs
    wide = own_ref[0].astype(jnp.float32)
    own = (wide[8:11] + wide[12:15]) + wide[16:19]
    centre = own[:, 0:1]
    upright = jnp.transpose(jnp.concatenate([own, jnp.zeros((5, LANES), jnp.float32)], 0))
    for k in range(3):
        column = (upright[:, k : k + 1] - centre[k : k + 1]) * SCALES[k]
        rows_ref[k] = jnp.broadcast_to(column, (LANES, LANES))
    member = lax.rem(lax.axis_index("grp"), PLANE_GROUPS)
    blocks = COL_CHUNK // LANES

    def tiles(cols, at):
        parts = []
        for col in cols:
            d = [rows_ref[k, pl.ds(at, ROW_CHUNK), :] - col[k] for k in range(3)]
            flat_q = d[0] * d[0] + d[1] * d[1]
            depth_q = d[2] * d[2]
            total = (flat_q + depth_q) + 1e-6
            scaled = total * lax.rsqrt(total)
            decay = jnp.exp2(math.log2(1.3) - scaled * math.log2(math.e))
            parts.append(((1.0 + scaled) * decay, flat_q * decay, depth_q * decay))
        return [jnp.concatenate([p[k] for p in parts], 1).astype(jnp.bfloat16) for k in range(3)]

    if first:
        total = jnp.zeros((8, 3 * LANES), jnp.float32)
    else:
        total = jnp.concatenate([before_ref[k] for k in range(3)], 1)
    slot = 0
    for offset in (-4, -2, 2, 4) if first else (-3, -1, 1, 3):
        wanted = member + offset
        group = lax.rem(wanted + PLANE_GROUPS, PLANE_GROUPS)
        inside = (wanted >= 0) & (wanted < PLANE_GROUPS)
        twin = lax.rem(group + 2, 4) + jnp.where(group < 4, 4, 0)
        place = jnp.where(inside, group, twin) // 2
        kind = jnp.where(group < 4, 1, 0)
        for part in range(ROW_TILES // blocks):
            cells = [
                unpack(far_ref[place * ROW_TILES + part * blocks + w], kind) for w in range(blocks)
            ]
            for half in range(2):
                probe = jnp.concatenate(
                    [cell[0][half * 8 : half * 8 + 8] for cell in cells], 1
                ).astype(jnp.bfloat16)
                cols = [
                    [
                        jnp.broadcast_to(
                            (cell[1][half * 3 + k : half * 3 + k + 1] - centre[k : k + 1])
                            * SCALES[k],
                            (ROW_CHUNK, LANES),
                        )
                        for k in range(3)
                    ]
                    for cell in cells
                ]
                for start in range(0, LANES, ROW_CHUNK):
                    made = tiles(cols, start)
                    for k in range(3):
                        tile_ref[slot % 4, pl.ds(k * LANES + start, ROW_CHUNK), :] = made[k]
                total = total + lax.dot_general(
                    probe,
                    tile_ref[slot % 4],
                    (((1,), (1,)), ((), ())),
                    preferred_element_type=jnp.float32,
                )
                slot += 1
    for k in range(3):
        out_ref[k] = total[:, k * LANES : (k + 1) * LANES]


def products(kernel, *operands):
    return pl.pallas_call(
        kernel,
        out_shape=jax.ShapeDtypeStruct((3, 8, LANES), jnp.float32),
        in_specs=[pl.BlockSpec(memory_space=pltpu.VMEM)] * len(operands),
        out_specs=pl.BlockSpec(memory_space=pltpu.VMEM),
        scratch_shapes=[
            pltpu.VMEM((3, LANES, LANES), jnp.float32),
            pltpu.VMEM((4, 3 * LANES, COL_CHUNK), jnp.bfloat16),
        ],
        compiler_params=pltpu.CompilerParams(vmem_limit_bytes=32 * 2**20),
        cost_estimate=pl.CostEstimate(flops=30_000_000, bytes_accessed=500_000, transcendentals=1_000_000),
    )(*operands)


def body(points, probes):
    own = pack(points, probes)
    same = within_plane(gather(across_planes(own)))
    same, early = lax.optimization_barrier((same, products(early_kernel, own, same)))
    swapped = other_core(same)
    half = products(late_kernel, own, same, early)
    return products(lambda *refs: products_kernel(False, *refs), own, swapped, half)


def solution(mesh):
    return jax.shard_map(
        body,
        mesh=mesh,
        in_specs=(P(None, ("grp", "tile")), P(None, ("grp", "tile"))),
        out_specs=P(None, None, ("grp", "tile")),
        check_vma=False,
    )
```

```python
import math

import jax
import jax.numpy as jnp
from jax import lax
from jax.experimental import pallas as pl
from jax.experimental.pallas import tpu as pltpu
from jax.sharding import PartitionSpec as P

ROUNDS = 4
PLANE_GROUPS = 8
PLANES = 16
ROW_TILES = 4
LANES = 128
ROWS = 24
SET_ROWS = 72
ROW_CHUNK = 16
COL_CHUNK = 512
SCALES = (math.sqrt(3) / 0.35, math.sqrt(3) / 0.35, math.sqrt(3) / 0.25)


def device_at(plane, member, column):
    return ((plane % 8) * PLANE_GROUPS + member) * 8 + (plane // 8) * ROW_TILES + column


def across_planes(copies):
    sets = []
    for plane in range(PLANES // 2):
        for member in range(4, PLANE_GROUPS):
            for column in range(ROW_TILES):
                lower = (member + 2) % 4
                near = [device_at(plane, member, column), device_at(plane + 1, lower, column)]
                far = [
                    device_at(plane + 8, member, column),
                    device_at((plane + 9) % PLANES, lower, column),
                ]
                sets.append(near + far if plane == 7 else far + near)
    return lax.all_to_all(copies, ("grp", "tile"), 0, 0, axis_index_groups=sets)


def within_plane(copies):
    planes = [
        [
            device_at(plane, 2 * m + core, c)
            for m in range(PLANE_GROUPS // 2)
            for c in (2, 3, 0, 1)
        ]
        for plane in range(PLANES)
        for core in range(2)
    ]
    return lax.all_to_all(copies, ("grp", "tile"), 0, 0, axis_index_groups=planes)


def other_core(block):
    return lax.ppermute(block, "grp", [(i, i ^ 1) for i in range(64)])


def pack_kernel(points_ref, probes_ref, out_ref):
    rest = points_ref[...]
    parts = []
    for _ in range(3):
        part = rest.astype(jnp.bfloat16).astype(jnp.float32)
        parts += [part, jnp.zeros((1, LANES), jnp.float32)]
        rest = rest - part
    probes = probes_ref[...].astype(jnp.float32)
    packed = jnp.concatenate(
        [probes] + parts + [jnp.zeros((4, LANES), jnp.float32)], 0
    ).astype(jnp.bfloat16)
    for copy in range(4):
        out_ref[copy] = packed


def pack(points, probes):
    points = pltpu.with_memory_space_constraint(points, pltpu.HBM)
    probes = pltpu.with_memory_space_constraint(probes, pltpu.HBM)
    return pl.pallas_call(
        pack_kernel,
        out_shape=jax.ShapeDtypeStruct((4, ROWS, LANES), jnp.bfloat16),
        in_specs=[pl.BlockSpec(memory_space=pltpu.VMEM)] * 2,
        out_specs=pl.BlockSpec(memory_space=pltpu.VMEM),
        compiler_params=pltpu.CompilerParams(vmem_limit_bytes=2**20),
    )(points, probes)


def gather_kernel(set_ref, out_ref):
    wide = [set_ref[b].astype(jnp.float32) for b in (0, 2, 1, 3)]
    packed = jnp.concatenate(
        [block[0:8] for block in wide]
        + [block[at : at + 3] for at in (8, 12, 16) for block in wide]
        + [jnp.zeros((4, LANES), jnp.float32)],
        0,
    ).astype(jnp.bfloat16)
    for copy in range(out_ref.shape[0]):
        out_ref[copy] = packed


def gather(blocks):
    return pl.pallas_call(
        gather_kernel,
        out_shape=jax.ShapeDtypeStruct((16, SET_ROWS, LANES), jnp.bfloat16),
        in_specs=[pl.BlockSpec(memory_space=pltpu.VMEM)],
        out_specs=pl.BlockSpec(memory_space=pltpu.VMEM),
        compiler_params=pltpu.CompilerParams(vmem_limit_bytes=2**20),
    )(blocks)


def unpack(message, kind):
    wide = message.astype(jnp.float32)
    coords = (wide[32:44] + wide[44:56]) + wide[56:68]
    first = kind == 0
    return jnp.where(first, wide[0:16], wide[16:32]), jnp.where(first, coords[0:6], coords[6:12])


def early_kernel(own_ref, far_ref, out_ref, rows_ref, tile_ref):
    core = lax.rem(lax.axis_index("grp"), 2)

    @pl.when(core == 1)
    def _():
        products_kernel(True, own_ref, far_ref, out_ref, rows_ref, tile_ref)

    @pl.when(core == 0)
    def _():
        out_ref[...] = jnp.zeros(out_ref.shape, jnp.float32)


def late_kernel(own_ref, far_ref, before_ref, out_ref, rows_ref, tile_ref):
    core = lax.rem(lax.axis_index("grp"), 2)

    @pl.when(core == 0)
    def _():
        products_kernel(True, own_ref, far_ref, out_ref, rows_ref, tile_ref)

    @pl.when(core == 1)
    def _():
        out_ref[...] = before_ref[...]


def products_kernel(first, *refs):
    if first:
        own_ref, far_ref, out_ref, rows_ref, tile_ref = refs
    else:
        own_ref, far_ref, before_ref, out_ref, rows_ref, tile_ref = refs
    wide = own_ref[0].astype(jnp.float32)
    own = (wide[8:11] + wide[12:15]) + wide[16:19]
    centre = own[:, 0:1]
    upright = jnp.transpose(jnp.concatenate([own, jnp.zeros((5, LANES), jnp.float32)], 0))
    for k in range(3):
        column = (upright[:, k : k + 1] - centre[k : k + 1]) * SCALES[k]
        rows_ref[k] = jnp.broadcast_to(column, (LANES, LANES))
    member = lax.rem(lax.axis_index("grp"), PLANE_GROUPS)
    blocks = COL_CHUNK // LANES

    def tiles(cols, at):
        parts = []
        for col in cols:
            d = [rows_ref[k, pl.ds(at, ROW_CHUNK), :] - col[k] for k in range(3)]
            flat_q = d[0] * d[0] + d[1] * d[1]
            depth_q = d[2] * d[2]
            total = (flat_q + depth_q) + 1e-6
            scaled = total * lax.rsqrt(total)
            decay = jnp.exp2(math.log2(1.3) - scaled * math.log2(math.e))
            parts.append(((1.0 + scaled) * decay, flat_q * decay, depth_q * decay))
        return [jnp.concatenate([p[k] for p in parts], 1).astype(jnp.bfloat16) for k in range(3)]

    if first:
        total = jnp.zeros((8, 3 * LANES), jnp.float32)
    else:
        total = jnp.concatenate([before_ref[k] for k in range(3)], 1)
    slot = 0
    for offset in (-4, -2, 2, 4) if first else (-3, -1, 1, 3):
        wanted = member + offset
        group = lax.rem(wanted + PLANE_GROUPS, PLANE_GROUPS)
        inside = (wanted >= 0) & (wanted < PLANE_GROUPS)
        twin = lax.rem(group + 2, 4) + jnp.where(group < 4, 4, 0)
        place = jnp.where(inside, group, twin) // 2
        kind = jnp.where(group < 4, 1, 0)
        for part in range(ROW_TILES // blocks):
            cells = [
                unpack(far_ref[place * ROW_TILES + part * blocks + w], kind) for w in range(blocks)
            ]
            for half in range(2):
                probe = jnp.concatenate(
                    [cell[0][half * 8 : half * 8 + 8] for cell in cells], 1
                ).astype(jnp.bfloat16)
                cols = [
                    [
                        jnp.broadcast_to(
                            (cell[1][half * 3 + k : half * 3 + k + 1] - centre[k : k + 1])
                            * SCALES[k],
                            (ROW_CHUNK, LANES),
                        )
                        for k in range(3)
                    ]
                    for cell in cells
                ]
                for start in range(0, LANES, ROW_CHUNK):
                    made = tiles(cols, start)
                    for k in range(3):
                        tile_ref[slot % 4, pl.ds(k * LANES + start, ROW_CHUNK), :] = made[k]
                total = total + lax.dot_general(
                    probe,
                    tile_ref[slot % 4],
                    (((1,), (1,)), ((), ())),
                    preferred_element_type=jnp.float32,
                )
                slot += 1
    for k in range(3):
        out_ref[k] = total[:, k * LANES : (k + 1) * LANES]


def products(kernel, *operands):
    return pl.pallas_call(
        kernel,
        out_shape=jax.ShapeDtypeStruct((3, 8, LANES), jnp.float32),
        in_specs=[pl.BlockSpec(memory_space=pltpu.VMEM)] * len(operands),
        out_specs=pl.BlockSpec(memory_space=pltpu.VMEM),
        scratch_shapes=[
            pltpu.VMEM((3, LANES, LANES), jnp.float32),
            pltpu.VMEM((4, 3 * LANES, COL_CHUNK), jnp.bfloat16),
        ],
        compiler_params=pltpu.CompilerParams(vmem_limit_bytes=32 * 2**20),
        cost_estimate=pl.CostEstimate(flops=30_000_000, bytes_accessed=500_000, transcendentals=1_000_000),
    )(*operands)


def body(points, probes):
    own = pack(points, probes)
    same = within_plane(gather(across_planes(own)))
    same, early = lax.optimization_barrier((same, products(early_kernel, own, same)))
    swapped = other_core(same)
    half = products(late_kernel, own, same, early)
    return products(lambda *refs: products_kernel(False, *refs), own, swapped, half)


def solution(mesh):
    return jax.shard_map(
        body,
        mesh=mesh,
        in_specs=(P(None, ("grp", "tile")), P(None, ("grp", "tile"))),
        out_specs=P(None, None, ("grp", "tile")),
        check_vma=False,
    )
```
